256 devices in a mesh: dp: 2 (over core), seq: 32 (over y, z_lo, x), heads: 4 (over z_hi).
Axes of the slice: x: 4, y: 4, z: 8 (z_hi: 4, z_lo: 2; z = z_hi * 2 + z_lo), core: 2. Of those that a mesh axis runs over, the one named last changes fastest.
Arguments:
- frames_in: bfloat16 [2, 32, 512, 2048], P('dp', 'seq'), may hold values from -80 to 80
- w_query: bfloat16 [2048, 2048], P(('dp', 'seq'), 'heads'), may hold values from -0.125 to 0.125
- w_key: bfloat16 [2048, 2048], P(('dp', 'seq'), 'heads'), may hold values from -0.125 to 0.125
- w_value: bfloat16 [2048, 2048], P(('dp', 'seq'), 'heads'), may hold values from -0.125 to 0.125
- w_out: bfloat16 [2048, 2048], P('heads', ('dp', 'seq')), may hold values from -0.125 to 0.125
- grad_in: bfloat16 [2, 32, 512, 2048], P('dp', 'seq'), may hold values from -6 to 6
Outputs:
- grad_frames: bfloat16 [2, 32, 512, 2048], P('dp', 'seq', None, 'heads')
- grad_query: bfloat16 [2048, 2048], P(('dp', 'seq'), 'heads')
- grad_key: bfloat16 [2048, 2048], P(('dp', 'seq'), 'heads')
- grad_value: bfloat16 [2048, 2048], P(('dp', 'seq'), 'heads')
- grad_out: bfloat16 [2048, 2048], P('heads', ('dp', 'seq'))
The draws below stay inside these ranges and needn't reach their ends.
All inputs are finite; a program needn't handle non-finite values.
Results may differ from the reference program's by a relative error of at most 0.018.
Values may be sent and summed in bfloat16 or wider, within the bound.
No kernel may reach another device: no remote copies, remote signals or barrier semaphores. Data moves between devices by JAX's collectives and lax.ppermute only.
A program may use at most 128 MiB of HBM per device.

```python
import math
import jax
import jax.numpy as jnp
from jax import lax

D = 2048
HEADS = 16
HD = 128
POS = 512
FRAMES = 32
VIDEOS = 2
TOKENS = 32768


def draw_frames_in(key, part):
    key = jax.random.fold_in(key, 11)
    base_key, row_key, col_key = jax.random.split(key, 3)
    shape = (VIDEOS, FRAMES, POS, D)
    base = jnp.clip(jax.random.normal(base_key, shape, jnp.float32), -4.0, 4.0)
    row_top = math.log(10.0)
    rows = jnp.exp(jax.random.uniform(row_key, (VIDEOS, FRAMES, POS, 1), jnp.float32, 0.0, row_top))
    cols = jnp.exp(jax.random.uniform(col_key, (1, 1, 1, D), jnp.float32, math.log(0.5), math.log(2.0)))
    values = jnp.clip(base * rows * cols, -80.0, 80.0)
    return values.astype(jnp.bfloat16)


def strengthened(result, rng, source, target, blocks, factor):
    owner, partner = [(jnp.arange(result.shape[dim]) // (result.shape[dim] // blocks)).reshape([-1 if axis == dim else 1 for axis in range(result.ndim)]) for dim in (source, target)]
    chosen = jax.random.permutation(rng, blocks)[partner]
    strong = (owner == chosen) | (owner == (partner + blocks // 2) % blocks)
    return jnp.where(strong, factor * result, result)


def levels(rng, extent, cuts, smallest, largest):
    factor_of = 1.0
    for axis_at, parts in cuts:
        draws = jax.random.uniform(jax.random.fold_in(jax.random.fold_in(rng, 6), axis_at), (parts,), jnp.float32, smallest / len(cuts), largest / len(cuts))
        factor_of = factor_of * jnp.repeat(jnp.exp(draws), extent[axis_at] // parts).reshape((-1,) + (1,) * (len(extent) - 1 - axis_at))
    return factor_of


def gaussian(stream_key, dims, width, bound, cuts=(), dtype=jnp.bfloat16):
    level = levels(stream_key, dims, cuts, -0.22, 0.18) if cuts else 1.0
    values = jax.random.normal(stream_key, dims, jnp.float32) * width * level
    return jnp.minimum(jnp.maximum(values, -bound), bound).astype(dtype)


def noise_with(rng, shape, deviation, reach, cuts, heavy, dtype=jnp.bfloat16):
    entries = deviation * jax.random.normal(rng, shape, jnp.float32)
    if cuts:
        entries = entries * levels(rng, shape, cuts, -0.22, 0.18)
    return jnp.clip(strengthened(entries, jax.random.fold_in(rng, 3), *heavy), -reach, reach).astype(dtype)


def setup_inputs(seed: int = 0) -> dict:
    seeds = jax.random.split(jax.random.key(seed), 7)
    return {
        "frames_in": draw_frames_in(jax.random.fold_in(seeds[6], 71), 0),
        "w_query": gaussian(seeds[1], (D, D), D ** -0.5, 0.125, ((0, 64), (1, 4))),
        "w_key": gaussian(seeds[2], (D, D), D ** -0.5, 0.125, ((0, 64), (1, 4))),
        "w_value": gaussian(seeds[3], (D, D), D ** -0.5, 0.125, ((0, 64), (1, 4))),
        "w_out": gaussian(seeds[4], (D, D), D ** -0.5, 0.125, ((0, 4), (1, 64))),
        "grad_in": noise_with(seeds[5], (VIDEOS, FRAMES, POS, D), 1.0, 6.0, ((0, 2), (1, 32)), (1, 3, 32, 2.75)),
    }


EPS = 1e-06

def norm_heads(t):
    split = t.reshape(t.shape[:-1] + (t.shape[-1] // HD, HD))
    scaled = split * lax.rsqrt(lax.optimization_barrier(jnp.mean(split * split, axis=-1, keepdims=True)) + EPS)
    return scaled.reshape(t.shape)

def one_video(feats, cots, w_query, w_key, w_value, w_out):
    flat = feats.reshape(FRAMES * POS, D)
    upstream = cots.reshape(FRAMES * POS, D)
    query = jnp.dot(flat, w_query, preferred_element_type=jnp.float32)
    key_raw = jnp.dot(flat, w_key, preferred_element_type=jnp.float32)
    value_raw = jnp.dot(flat, w_value, preferred_element_type=jnp.float32)
    shape4 = (FRAMES, POS, HEADS, HD)
    normq = norm_heads(query).astype(jnp.bfloat16).reshape(shape4).astype(jnp.float32)
    normk = norm_heads(key_raw).astype(jnp.bfloat16).reshape(shape4).astype(jnp.float32)
    value_b = value_raw.astype(jnp.bfloat16).reshape(shape4).astype(jnp.float32)
    factor = HD ** (-0.5)
    scores = jnp.einsum('fphe,gphe->phfg', normq, normk) * factor
    weights = jnp.exp(scores)
    probs = weights / lax.optimization_barrier(jnp.sum(weights, axis=-1, keepdims=True))
    probs_b = probs.astype(jnp.bfloat16).astype(jnp.float32)
    attended = jnp.einsum('phfg,gphe->fphe', probs_b, value_b).astype(jnp.bfloat16).reshape(FRAMES * POS, D)
    grad_att = lax.dot_general(upstream, w_out, (((1,), (1,)), ((), ())), preferred_element_type=jnp.float32)
    grad_att = grad_att.astype(jnp.bfloat16).reshape(shape4).astype(jnp.float32)
    dprobs = jnp.einsum('fphe,gphe->phfg', grad_att, value_b)
    delta = lax.optimization_barrier(jnp.sum(probs * dprobs, axis=-1, keepdims=True))
    dscores = (probs * (dprobs - delta)).astype(jnp.bfloat16).astype(jnp.float32)
    dnormq = (jnp.einsum('phfg,gphe->fphe', dscores, normk) * factor).astype(jnp.bfloat16)
    dnormk = (jnp.einsum('phfg,fphe->gphe', dscores, normq) * factor).astype(jnp.bfloat16)
    dvalue = jnp.einsum('phfg,fphe->gphe', probs_b, grad_att).astype(jnp.bfloat16).reshape(FRAMES * POS, D)
    back_q = jax.vjp(norm_heads, query)[1]
    back_k = jax.vjp(norm_heads, key_raw)[1]
    dquery = back_q(dnormq.reshape(FRAMES * POS, D).astype(jnp.float32))[0].astype(jnp.bfloat16)
    dkey = back_k(dnormk.reshape(FRAMES * POS, D).astype(jnp.float32))[0].astype(jnp.bfloat16)
    contract_cols = (((1,), (1,)), ((), ()))
    grad_x = lax.dot_general(dquery, w_query, contract_cols, preferred_element_type=jnp.float32)
    grad_x = grad_x + lax.dot_general(dkey, w_key, contract_cols, preferred_element_type=jnp.float32)
    grad_x = grad_x + lax.dot_general(dvalue, w_value, contract_cols, preferred_element_type=jnp.float32)
    grad_x = grad_x.astype(jnp.bfloat16).reshape(FRAMES, POS, D)
    contract_rows = (((0,), (0,)), ((), ()))
    term_q = lax.dot_general(flat, dquery, contract_rows, preferred_element_type=jnp.float32)
    term_k = lax.dot_general(flat, dkey, contract_rows, preferred_element_type=jnp.float32)
    term_v = lax.dot_general(flat, dvalue, contract_rows, preferred_element_type=jnp.float32)
    term_o = lax.dot_general(attended, upstream, contract_rows, preferred_element_type=jnp.float32)
    return (grad_x, term_q, term_k, term_v, term_o)

def reference(frames_in, w_query, w_key, w_value, w_out, grad_in):
    grads = []
    total_q = jnp.zeros((D, D), jnp.float32)
    total_k = jnp.zeros((D, D), jnp.float32)
    total_v = jnp.zeros((D, D), jnp.float32)
    total_o = jnp.zeros((D, D), jnp.float32)
    for video in range(VIDEOS):
        grad_x, term_q, term_k, term_v, term_o = one_video(frames_in[video], grad_in[video], w_query, w_key, w_value, w_out)
        grads.append(grad_x)
        total_q = total_q + term_q
        total_k = total_k + term_k
        total_v = total_v + term_v
        total_o = total_o + term_o
    gscale = TOKENS ** (-0.5)
    grad_frames = jnp.stack(grads, axis=0)
    return (grad_frames, (total_q * gscale).astype(jnp.bfloat16), (total_k * gscale).astype(jnp.bfloat16), (total_v * gscale).astype(jnp.bfloat16), (total_o * gscale).astype(jnp.bfloat16))
```

```python
import functools

import jax
import jax.numpy as jnp
from jax import lax
from jax.experimental import pallas as pl
from jax.experimental.pallas import tpu as pltpu
from jax.sharding import Mesh
from jax.sharding import PartitionSpec as P

HD = 128
EPS = 1e-06
FACTOR = HD ** (-0.5)
SEQ = ("y", "z", "x")
OFFSETS = (0, -1, 1, 2)
BF16 = jnp.bfloat16
F32 = jnp.float32
VMEM = pl.BlockSpec(memory_space=pltpu.VMEM)
ANY = pl.BlockSpec(memory_space=pl.ANY)
LIMIT = 60 * 1024 * 1024


def dot(left, right, dims):
    return lax.dot_general(left, right, (dims, ((), ())), preferred_element_type=F32)


def normed(t):
    scale = lax.rsqrt(jnp.mean(t * t, axis=-1, keepdims=True) + EPS)
    return t * scale, scale


def norm_back(n, scale, grad):
    return scale * (grad - n * jnp.mean(n * grad, axis=-1, keepdims=True))


def attention(q, k, v, g, same):
    nq, rq = normed(q)
    nk, rk = normed(k)
    nqb, nkb, vb, gb = nq.astype(BF16), nk.astype(BF16), v.astype(BF16), g.astype(BF16)
    scores = dot(nqb, nkb, ((1,), (1,))) * FACTOR
    weights = jnp.where(same, jnp.exp(scores), 0.0)
    probs = weights / jnp.sum(weights, axis=-1, keepdims=True)
    probs_b = probs.astype(BF16)
    att = dot(probs_b, vb, ((1,), (0,)))
    dprobs = dot(gb, vb, ((1,), (1,)))
    weighted = probs * dprobs
    delta = jnp.sum(weighted, axis=-1, keepdims=True)
    dscores = (weighted - probs * delta).astype(BF16)
    dnq = dot(dscores, nkb, ((1,), (0,))) * FACTOR
    dnk = dot(dscores, nqb, ((0,), (0,))) * FACTOR
    dv = dot(probs_b, gb, ((0,), (0,)))
    return norm_back(nq, rq, dnq), norm_back(nk, rk, dnk), dv, att


def main_kernel(place, x0, x1, u0, u1, *refs):
    pieces, (t0, t1, d0, d1), (w, proj, back, sems) = refs[:10], refs[10:14], refs[14:]
    y, x = place[0], place[1]
    copies = []

    def fetch(src, dst):
        copies.append(pltpu.make_async_copy(src, dst, sems.at[len(copies)]))
        copies[-1].start()

    for half in range(2):
        own, before, after, far_a, far_b = pieces[5 * half : 5 * half + 5]
        for i, outer in enumerate(OFFSETS):
            for j, inner in enumerate(OFFSETS):
                if i < 3:
                    src = (own, before, after)[i].at[j]
                else:
                    src = (far_a if j < 2 else far_b).at[j % 2]
                yy, xx = (inner, outer) if half == 0 else (outer, inner)
                fetch(src, w.at[half, lax.rem(y + yy + 4, 4), :, lax.rem(x + xx + 4, 4)])
    for copy in copies:
        copy.wait()

    row = lax.broadcasted_iota(jnp.int32, (256, 256), 0)
    col = lax.broadcasted_iota(jnp.int32, (256, 256), 1)
    same = lax.rem(row, 8) == lax.rem(col, 8)
    for x_in, u_in, t_out, d_out in ((x0, u0, t0, d0), (x1, u1, t1, d1)):
        for kind in range(4):
            tokens = (u_in if kind == 3 else x_in)[...].reshape(512, 2048)
            cols = slice(kind * 256, kind * 256 + 256)
            acc = dot(tokens[:, :1024], w[0, :, :, :, :, cols].reshape(1024, 256), ((1,), (0,)))
            acc += dot(tokens[:, 1024:], w[1, :, :, :, :, cols].reshape(1024, 256), ((1,), (0,)))
            proj[:, :, :, cols] = acc.reshape(32, 2, 8, 256)
        for head in range(2):
            for part in range(2):
                at = [kind * 256 + head * 128 for kind in range(4)]
                out = attention(*(proj[:, part, :, a : a + 128].reshape(256, 128) for a in at), same)
                for a, value in zip(at, out):
                    back[:, part, :, a : a + 128] = value.reshape(32, 8, 128)
        d_all = back[...].reshape(512, 1024).astype(BF16)
        d_out[...] = d_all
        for chunk in range(4):
            half, first = chunk // 2, 2 * (chunk % 2)
            rows = w[half, first : first + 2, :, :, :, :768].reshape(512, 768)
            t_out[chunk] = dot(d_all[:, :768], rows, ((1,), (1,))).astype(BF16)


def grads_kernel(x0, x1, u0, u1, d0, d1, out):
    for block in range(8):
        half, s = block // 4, 8 * (block % 4)
        cols = slice(block * 256, block * 256 + 256)
        for a, b, lo, hi in ((x0, x1, 0, 768), (u0, u1, 768, 1024)):
            acc = dot(a[:, :, cols].reshape(512, 256), d0[:, lo:hi], ((0,), (0,)))
            acc += dot(b[:, :, cols].reshape(512, 256), d1[:, lo:hi], ((0,), (0,)))
            out[s : s + 8, half, :, lo:hi] = acc.reshape(8, 32, hi - lo).astype(BF16)


def shift(t, axis, by):
    n = lax.axis_size(axis)
    return lax.ppermute(t, axis, [(i, (i + by) % n) for i in range(n)])


def ring(t, axis):
    before, after = shift(t, axis, 1), shift(t, axis, -1)
    half = t.shape[0] // 2
    return t, before, after, shift(before[:half], axis, 1), shift(after[half:], axis, -1)


def stacked(blocks):
    own, before, after, far_a, far_b = blocks
    return jnp.stack([own, before, after, jnp.concatenate([far_a, far_b], axis=0)])


def exchange(t, axis):
    return lax.all_to_all(t, axis, 0, 0, tiled=True)


def gathered(w_query, w_key, w_value, w_out):
    w = jnp.stack([w_query, w_key, w_value, w_out.T], axis=1)
    w = w.reshape(32, 4, 2, 256).transpose(2, 0, 1, 3).reshape(2, 32, 1024)
    w = exchange(w, "dp")
    other = shift(w, "z", 1)
    low = lax.axis_index("z") == 0
    pair = jnp.stack([jnp.where(low, w, other), jnp.where(low, other, w)], axis=1)
    first = ring(stacked(ring(pair[0], "y")), "x")
    second = ring(stacked(ring(pair[1], "x")), "y")
    return first + second


def on_device(frames_in, w_query, w_key, w_value, w_out, grad_in):
    x0 = exchange(frames_in.reshape(32, 16, 2048), SEQ)
    u0 = exchange(grad_in.reshape(32, 16, 2048), SEQ)
    pieces = gathered(w_query, w_key, w_value, w_out)
    x1 = shift(x0, "dp", 1)
    u1 = shift(u0, "dp", 1)
    place = jnp.stack([lax.axis_index("y"), lax.axis_index("x")]).astype(jnp.int32)
    t0, t1, d0, d1 = pl.pallas_call(
        main_kernel,
        out_shape=[jax.ShapeDtypeStruct((4, 512, 512), BF16)] * 2
        + [jax.ShapeDtypeStruct((512, 1024), BF16)] * 2,
        in_specs=[pl.BlockSpec(memory_space=pltpu.SMEM)] + [VMEM] * 4 + [ANY] * 10,
        out_specs=[VMEM] * 4,
        scratch_shapes=[
            pltpu.VMEM((2, 4, 2, 4, 32, 1024), BF16),
            pltpu.VMEM((32, 2, 8, 1024), F32),
            pltpu.VMEM((32, 2, 8, 1024), F32),
            pltpu.SemaphoreType.DMA((32,)),
        ],
        compiler_params=pltpu.CompilerParams(vmem_limit_bytes=LIMIT),
        cost_estimate=pl.CostEstimate(flops=9_000_000_000, bytes_accessed=18 << 20, transcendentals=1 << 19),
    )(place, x0, x1, u0, u1, *pieces)
    term = t0.astype(F32) + shift(t1, "dp", 1).astype(F32)
    mine = lax.psum_scatter(term.astype(BF16), "heads", scatter_dimension=0, tiled=True)
    grad_frames = exchange(mine.reshape(32, 16, 512), SEQ).reshape(1, 1, 512, 512)
    grads = pl.pallas_call(
        grads_kernel,
        out_shape=jax.ShapeDtypeStruct((32, 2, 32, 1024), BF16),
        in_specs=[VMEM] * 6,
        out_specs=VMEM,
        compiler_params=pltpu.CompilerParams(vmem_limit_bytes=LIMIT),
        cost_estimate=pl.CostEstimate(flops=4_300_000_000, bytes_accessed=14 << 20, transcendentals=0),
    )(x0, x1, u0, u1, d0, d1)
    gscale = 32768 ** (-0.5)
    sums = jnp.sum(exchange(grads, SEQ).astype(F32), axis=0) * gscale
    sums = exchange(sums.astype(BF16), "dp").reshape(2, 32, 4, 256)
    gq, gk, gv, go = (
        jnp.concatenate([sums[0, :, kind], sums[1, :, kind]], axis=1) for kind in range(4)
    )
    return grad_frames, gq, gk, gv, go.T


def solution(mesh):
    fine = Mesh(mesh.devices.reshape(2, 4, 2, 4, 4), ("dp", "y", "z", "x", "heads"))
    tokens = P("dp", SEQ, None, None)
    rows = P(("dp",) + SEQ, "heads")
    cols = P("heads", ("dp",) + SEQ)
    return jax.shard_map(
        on_device,
        mesh=fine,
        in_specs=(tokens, rows, rows, rows, cols, tokens),
        out_specs=(P("dp", SEQ, None, "heads"), rows, rows, rows, cols),
        check_vma=False,
    )
```

```python
import functools

import jax
import jax.numpy as jnp
from jax import lax
from jax.experimental import pallas as pl
from jax.experimental.pallas import tpu as pltpu
from jax.sharding import Mesh
from jax.sharding import PartitionSpec as P

HD = 128
EPS = 1e-06
FACTOR = HD ** (-0.5)
SEQ = ("y", "z", "x")
OFFSETS = (0, -1, 1, 2)
BF16 = jnp.bfloat16
F32 = jnp.float32
VMEM = pl.BlockSpec(memory_space=pltpu.VMEM)
ANY = pl.BlockSpec(memory_space=pl.ANY)
LIMIT = 60 * 1024 * 1024


def dot(left, right, dims):
    return lax.dot_general(left, right, (dims, ((), ())), preferred_element_type=F32)


def normed(t):
    scale = lax.rsqrt(jnp.mean(t * t, axis=-1, keepdims=True) + EPS)
    return t * scale, scale


def norm_back(n, scale, grad):
    return scale * (grad - n * jnp.mean(n * grad, axis=-1, keepdims=True))


def attention(q, k, v, g, same):
    nq, rq = normed(q)
    nk, rk = normed(k)
    nqb, nkb, vb, gb = nq.astype(BF16), nk.astype(BF16), v.astype(BF16), g.astype(BF16)
    scores = dot(nqb, nkb, ((1,), (1,))) * FACTOR
    weights = jnp.where(same, jnp.exp(scores), 0.0)
    probs = weights / jnp.sum(weights, axis=-1, keepdims=True)
    probs_b = probs.astype(BF16)
    att = dot(probs_b, vb, ((1,), (0,)))
    dprobs = dot(gb, vb, ((1,), (1,)))
    weighted = probs * dprobs
    delta = jnp.sum(weighted, axis=-1, keepdims=True)
    dscores = (weighted - probs * delta).astype(BF16)
    dnq = dot(dscores, nkb, ((1,), (0,))) * FACTOR
    dnk = dot(dscores, nqb, ((0,), (0,))) * FACTOR
    dv = dot(probs_b, gb, ((0,), (0,)))
    return norm_back(nq, rq, dnq), norm_back(nk, rk, dnk), dv, att


def main_kernel(place, x_in, u_in, *refs):
    pieces, (t_out, d_out), (w, proj, back, sems) = refs[:10], refs[10:12], refs[12:]
    y, x = place[0], place[1]
    copies = []

    def fetch(src, dst):
        copies.append(pltpu.make_async_copy(src, dst, sems.at[len(copies)]))
        copies[-1].start()

    for half in range(2):
        own, before, after, far_a, far_b = pieces[5 * half : 5 * half + 5]
        for i, outer in enumerate(OFFSETS):
            for j, inner in enumerate(OFFSETS):
                if i < 3:
                    src = (own, before, after)[i].at[j]
                else:
                    src = (far_a if j < 2 else far_b).at[j % 2]
                yy, xx = (inner, outer) if half == 0 else (outer, inner)
                fetch(src, w.at[half, lax.rem(y + yy + 4, 4), :, lax.rem(x + xx + 4, 4)])
    for copy in copies:
        copy.wait()

    row = lax.broadcasted_iota(jnp.int32, (256, 256), 0)
    col = lax.broadcasted_iota(jnp.int32, (256, 256), 1)
    same = lax.rem(row, 8) == lax.rem(col, 8)
    for kind in range(4):
        tokens = (u_in if kind == 3 else x_in)[...].reshape(512, 2048)
        cols = slice(kind * 256, kind * 256 + 256)
        acc = dot(tokens[:, :1024], w[0, :, :, :, :, cols].reshape(1024, 256), ((1,), (0,)))
        acc += dot(tokens[:, 1024:], w[1, :, :, :, :, cols].reshape(1024, 256), ((1,), (0,)))
        proj[:, :, :, cols] = acc.reshape(32, 2, 8, 256)
    for head in range(2):
        for part in range(2):
            at = [kind * 256 + head * 128 for kind in range(4)]
            out = attention(*(proj[:, part, :, a : a + 128].reshape(256, 128) for a in at), same)
            for a, value in zip(at, out):
                back[:, part, :, a : a + 128] = value.reshape(32, 8, 128)
    d_all = back[...].reshape(512, 1024).astype(BF16)
    d_out[...] = d_all
    for chunk in range(4):
        half, first = chunk // 2, 2 * (chunk % 2)
        rows = w[half, first : first + 2, :, :, :, :768].reshape(512, 768)
        t_out[chunk] = dot(d_all[:, :768], rows, ((1,), (1,))).astype(BF16)


def grads_kernel(place, x0, x1, u0, u1, d0, d1, *refs):
    outs, full = refs[:8], refs[8]
    for block in range(8):
        half, y = block // 4, block % 4
        cols = slice(block * 256, block * 256 + 256)
        for a, b, lo, hi in ((x0, x1, 0, 768), (u0, u1, 768, 1024)):
            acc = dot(a[:, :, cols].reshape(512, 256), d0[:, lo:hi], ((0,), (0,)))
            acc += dot(b[:, :, cols].reshape(512, 256), d1[:, lo:hi], ((0,), (0,)))
            full[half, y, :, :, :, lo:hi] = acc.reshape(2, 4, 32, hi - lo).astype(BF16)
    for k, offset in enumerate(OFFSETS):
        outs[k][...] = full[0, :, :, lax.rem(place[1] + offset + 4, 4)]
        chosen = lax.rem(place[0] + offset + 4, 4)
        for x in range(4):
            outs[4 + k][x] = full[1, chosen, :, x]


def sum_kernel(place, *refs):
    for half in range(2):
        blocks, outs = refs[4 * half : 4 * half + 4], refs[8 + 4 * half : 12 + 4 * half]
        for k, offset in enumerate(OFFSETS):
            at = lax.rem(place[half] + offset + 4, 4)
            outs[k][...] = sum(block[at].astype(F32) for block in blocks).astype(BF16)


def last_kernel(place, *refs):
    keep, send = refs[8:]
    for half in range(2):
        blocks = refs[4 * half : 4 * half + 4]
        keep[half] = sum(block[place[2]].astype(F32) for block in blocks)
        send[half] = sum(block[1 - place[2]].astype(F32) for block in blocks).astype(BF16)


def add_kernel(place, a, b, near, after, before, far_a, far_b):
    def chunk(offset, rows):
        at = lax.rem(place[3] + offset + 4, 4)
        return (a[at, rows].astype(F32) + b[at, rows].astype(F32)).astype(BF16)

    every, top, low = slice(0, 512), slice(0, 256), slice(256, 512)
    near[...], after[...], before[...] = chunk(0, every), chunk(1, every), chunk(-1, every)
    far_a[...], far_b[...] = chunk(2, top), chunk(2, low)


def shift(t, axis, by):
    n = lax.axis_size(axis)
    return lax.ppermute(t, axis, [(i, (i + by) % n) for i in range(n)])


def ring(t, axis):
    before, after = shift(t, axis, 1), shift(t, axis, -1)
    half = t.shape[0] // 2
    return t, before, after, shift(before[:half], axis, 1), shift(after[half:], axis, -1)


def stacked(blocks):
    own, before, after, far_a, far_b = blocks
    return jnp.stack([own, before, after, jnp.concatenate([far_a, far_b], axis=0)])


def exchange(t, axis):
    return lax.all_to_all(t, axis, 0, 0, tiled=True)


def main(place, tokens, cots, pieces):
    return pl.pallas_call(
        main_kernel,
        out_shape=[
            jax.ShapeDtypeStruct((4, 512, 512), BF16),
            jax.ShapeDtypeStruct((512, 1024), BF16),
        ],
        in_specs=[pl.BlockSpec(memory_space=pltpu.SMEM)] + [VMEM] * 2 + [ANY] * 10,
        out_specs=[VMEM] * 2,
        scratch_shapes=[
            pltpu.VMEM((2, 4, 2, 4, 32, 1024), BF16),
            pltpu.VMEM((32, 2, 8, 1024), F32),
            pltpu.VMEM((32, 2, 8, 1024), F32),
            pltpu.SemaphoreType.DMA((32,)),
        ],
        compiler_params=pltpu.CompilerParams(vmem_limit_bytes=LIMIT),
        cost_estimate=pl.CostEstimate(flops=9_000_000_000, bytes_accessed=11 << 20, transcendentals=1 << 18),
    )(place, tokens, cots, *pieces)


def local(kernel, shapes, flops, nbytes, scratch=(), kinds=None):
    kinds = kinds or (BF16,) * len(shapes)

    def call(place, *arrays):
        return pl.pallas_call(
            kernel,
            out_shape=[jax.ShapeDtypeStruct(s, d) for s, d in zip(shapes, kinds)],
            in_specs=[pl.BlockSpec(memory_space=pltpu.SMEM)] + [VMEM] * len(arrays),
            out_specs=[VMEM] * len(shapes),
            scratch_shapes=list(scratch),
            compiler_params=pltpu.CompilerParams(vmem_limit_bytes=LIMIT),
            cost_estimate=pl.CostEstimate(flops=flops, bytes_accessed=nbytes, transcendentals=0),
        )(place, *arrays)

    return call


def plus(*terms):
    return sum(t.astype(F32) for t in terms).astype(BF16)


def swapped(blocks, axis):
    return [blocks[0]] + [shift(b, axis, o) for b, o in zip(blocks[1:], OFFSETS[1:])]


def on_device(frames_in, w_query, w_key, w_value, w_out, grad_in):
    together = lax.optimization_barrier
    first_core = lax.axis_index("dp") == 0
    w = jnp.stack([w_query, w_key, w_value, w_out.T], axis=1)
    w = w.reshape(32, 4, 2, 256).transpose(2, 0, 1, 3).reshape(2, 32, 1024)
    own = jnp.where(first_core, w[0], w[1])
    other = shift(jnp.where(first_core, w[1], w[0]), "dp", 1)
    w = jnp.stack([jnp.where(first_core, own, other), jnp.where(first_core, other, own)])
    other = shift(w, "z", 1)
    low = lax.axis_index("z") == 0
    pair = jnp.stack([jnp.where(low, w, other), jnp.where(low, other, w)], axis=1)
    first, second = stacked(ring(pair[0], "y")), stacked(ring(pair[1], "x"))
    u0 = exchange(grad_in.reshape(32, 16, 2048), SEQ)
    u0, first, second, frames_in = together((u0, first, second, frames_in))

    x0 = exchange(frames_in.reshape(32, 16, 2048), SEQ)
    u1 = shift(u0, "dp", 1)
    pieces = ring(first, "x") + ring(second, "y")
    x0, u1, pieces = together((x0, u1, pieces))

    x1 = shift(x0, "dp", 1)
    place = jnp.stack([lax.axis_index(a) for a in ("y", "x", "z", "heads")]).astype(jnp.int32)
    t0, d0 = main(place, x0, u0, pieces)
    x1, t0 = together((x1, t0))
    t1, d1 = main(place, x1, u1, pieces)

    t1 = shift(t1, "dp", 1)
    near, after, before, far_a, far_b = local(
        add_kernel, [(512, 512)] * 3 + [(256, 512)] * 2, 1 << 22, 6 << 20
    )(place, t0, t1)
    from_before, from_after = shift(far_a, "heads", 1), shift(far_b, "heads", -1)
    after = plus(after, jnp.pad(from_before, ((0, 256), (0, 0))))
    before = plus(before, jnp.pad(from_after, ((256, 0), (0, 0))))
    mine = plus(near, shift(after, "heads", 1), shift(before, "heads", -1))
    grad_frames = exchange(mine.reshape(32, 16, 512), SEQ).reshape(1, 1, 512, 512)

    blocks = local(
        grads_kernel,
        [(4, 2, 32, 1024)] * 8,
        9_000_000_000,
        14 << 20,
        [pltpu.VMEM((2, 4, 2, 4, 32, 1024), BF16)],
    )(place, x0, x1, u0, u1, d0, d1)
    blocks = swapped(blocks[:4], "x") + swapped(blocks[4:], "y")
    blocks = local(sum_kernel, [(2, 32, 1024)] * 8, 1 << 22, 5 << 20)(place, *blocks)
    blocks = swapped(blocks[:4], "y") + swapped(blocks[4:], "x")
    keep, send = local(last_kernel, [(2, 32, 1024)] * 2, 1 << 20, 1 << 20, kinds=(F32, BF16))(place, *blocks)
    sums = (keep + shift(send, "z", 1).astype(F32)) * 32768 ** (-0.5)
    sums = sums.astype(BF16)
    own = jnp.where(first_core, sums[0], sums[1])
    other = shift(jnp.where(first_core, sums[1], sums[0]), "dp", 1)
    sums = jnp.stack([jnp.where(first_core, own, other), jnp.where(first_core, other, own)])
    sums = sums.reshape(2, 32, 4, 256).transpose(2, 1, 0, 3).reshape(4, 32, 512)
    return grad_frames, sums[0], sums[1], sums[2], sums[3].T


def solution(mesh):
    fine = Mesh(mesh.devices.reshape(2, 4, 2, 4, 4), ("dp", "y", "z", "x", "heads"))
    tokens = P("dp", SEQ, None, None)
    rows = P(("dp",) + SEQ, "heads")
    cols = P("heads", ("dp",) + SEQ)
    return jax.shard_map(
        on_device,
        mesh=fine,
        in_specs=(tokens, rows, rows, rows, cols, tokens),
        out_specs=(P("dp", SEQ, None, "heads"), rows, rows, rows, cols),
        check_vma=False,
    )
```

```python
import functools

import jax
import jax.numpy as jnp
from jax import lax
from jax.experimental import pallas as pl
from jax.experimental.pallas import tpu as pltpu
from jax.sharding import Mesh
from jax.sharding import PartitionSpec as P

HD = 128
EPS = 1e-06
FACTOR = HD ** (-0.5)
SEQ = ("y", "z", "x")
OFFSETS = (0, -1, 1, 2)
BF16 = jnp.bfloat16
F32 = jnp.float32
VMEM = pl.BlockSpec(memory_space=pltpu.VMEM)
HBM = pl.BlockSpec(memory_space=pltpu.HBM)
LIMIT = 60 * 1024 * 1024


def dot(left, right, dims):
    return lax.dot_general(left, right, (dims, ((), ())), preferred_element_type=F32)


def normed(t):
    scale = lax.rsqrt(jnp.mean(t * t, axis=-1, keepdims=True) + EPS)
    return t * scale, scale


def norm_back(n, scale, grad):
    return scale * (grad - n * jnp.mean(n * grad, axis=-1, keepdims=True))


def attention(q, k, v, g, same):
    nq, rq = normed(q)
    nk, rk = normed(k)
    nqb, nkb, vb, gb = nq.astype(BF16), nk.astype(BF16), v.astype(BF16), g.astype(BF16)
    scores = dot(nqb, nkb, ((1,), (1,))) * FACTOR
    weights = jnp.where(same, jnp.exp(scores), 0.0)
    probs = weights / jnp.sum(weights, axis=-1, keepdims=True)
    probs_b = probs.astype(BF16)
    att = dot(probs_b, vb, ((1,), (0,)))
    dprobs = dot(gb, vb, ((1,), (1,)))
    weighted = probs * dprobs
    delta = jnp.sum(weighted, axis=-1, keepdims=True)
    dscores = (weighted - probs * delta).astype(BF16)
    dnq = dot(dscores, nkb, ((1,), (0,))) * FACTOR
    dnk = dot(dscores, nqb, ((0,), (0,))) * FACTOR
    dv = dot(probs_b, gb, ((0,), (0,)))
    return norm_back(nq, rq, dnq), norm_back(nk, rk, dnk), dv, att


def main_kernel(place, x_in, u_in, *refs):
    pieces, (t_out, d_out), (w, proj, back, sems) = refs[:10], refs[10:12], refs[12:]
    y, x = place[0], place[1]
    copies = []

    def fetch(src, dst):
        copies.append(pltpu.make_async_copy(src, dst, sems.at[len(copies)]))
        copies[-1].start()

    for half in range(2):
        own, before, after, far_a, far_b = pieces[5 * half : 5 * half + 5]
        for i, outer in enumerate(OFFSETS):
            for j, inner in enumerate(OFFSETS):
                if i < 3:
                    src = (own, before, after)[i].at[j]
                else:
                    src = (far_a if j < 2 else far_b).at[j % 2]
                yy, xx = (inner, outer) if half == 0 else (outer, inner)
                fetch(src, w.at[half, lax.rem(y + yy + 4, 4), :, lax.rem(x + xx + 4, 4)])
    for copy in copies:
        copy.wait()

    row = lax.broadcasted_iota(jnp.int32, (256, 256), 0)
    col = lax.broadcasted_iota(jnp.int32, (256, 256), 1)
    same = lax.rem(row, 8) == lax.rem(col, 8)
    for kind in range(4):
        tokens = (u_in if kind == 3 else x_in)[...].reshape(512, 2048)
        cols = slice(kind * 256, kind * 256 + 256)
        acc = dot(tokens[:, :1024], w[0, :, :, :, :, cols].reshape(1024, 256), ((1,), (0,)))
        acc += dot(tokens[:, 1024:], w[1, :, :, :, :, cols].reshape(1024, 256), ((1,), (0,)))
        proj[:, :, :, cols] = acc.reshape(32, 2, 8, 256)
    for head in range(2):
        for part in range(2):
            at = [kind * 256 + head * 128 for kind in range(4)]
            out = attention(*(proj[:, part, :, a : a + 128].reshape(256, 128) for a in at), same)
            for a, value in zip(at, out):
                back[:, part, :, a : a + 128] = value.reshape(32, 8, 128)
    d_all = back[...].reshape(512, 1024).astype(BF16)
    d_out[...] = d_all
    for chunk in range(4):
        half, first = chunk // 2, 2 * (chunk % 2)
        rows = w[half, first : first + 2, :, :, :, :768].reshape(512, 768)
        t_out[chunk] = dot(d_all[:, :768], rows, ((1,), (1,))).astype(BF16)


def grads_block(place, x0, x1, u0, u1, d0, d1, cols):
    for a, b, lo, hi in ((x0, x1, 0, 768), (u0, u1, 768, 1024)):
        acc = dot(a[:, :, cols].reshape(512, 256), d0[:, lo:hi], ((0,), (0,)))
        acc += dot(b[:, :, cols].reshape(512, 256), d1[:, lo:hi], ((0,), (0,)))
        yield lo, hi, acc.reshape(2, 4, 32, hi - lo).astype(BF16)


def first_kernel(place, *refs):
    outs, full = refs[6:11], refs[11]
    for y in range(4):
        for lo, hi, rows in grads_block(place, *refs[:6], slice(y * 256, y * 256 + 256)):
            full[y, :, :, :, lo:hi] = rows
    for k in range(3):
        outs[k][...] = full[:, :, lax.rem(place[1] + OFFSETS[k] + 4, 4)]
    far = lax.rem(place[1] + 2, 4)
    outs[3][...] = full[:2, :, far]
    outs[4][...] = full[2:, :, far]


def second_kernel(place, *refs):
    outs = refs[6:11]
    for k, offset in enumerate(OFFSETS):
        start = 1024 + 256 * lax.rem(place[0] + offset + 4, 4)
        for lo, hi, rows in grads_block(place, *refs[:6], pl.ds(pl.multiple_of(start, 256), 256)):
            for x in range(4):
                out = outs[k].at[x] if k < 3 else outs[3 + x // 2].at[x % 2]
                out[:, :, lo:hi] = rows[:, x]


def far_kernel(place, *refs):
    for half in range(2):
        before, after, far_a, far_b = refs[4 * half : 4 * half + 4]
        before_out, after_out = refs[8 + 2 * half : 10 + 2 * half]
        after_out[:2] = (after[:2].astype(F32) + far_a[...].astype(F32)).astype(BF16)
        after_out[2:] = after[2:]
        before_out[:2] = before[:2]
        before_out[2:] = (before[2:].astype(F32) + far_b[...].astype(F32)).astype(BF16)


def sum_kernel(place, *refs):
    for half in range(2):
        blocks, outs = refs[3 * half : 3 * half + 3], refs[6 + 4 * half : 10 + 4 * half]
        for k, offset in enumerate(OFFSETS):
            at = lax.rem(place[half] + offset + 4, 4)
            outs[k][...] = sum(block[at].astype(F32) for block in blocks).astype(BF16)


def last_kernel(place, *refs):
    keep, send = refs[8:]
    for half in range(2):
        blocks = refs[4 * half : 4 * half + 4]
        keep[half] = sum(block[place[2]].astype(F32) for block in blocks)
        send[half] = sum(block[1 - place[2]].astype(F32) for block in blocks).astype(BF16)


def finish_kernel(place, own, other, *outs):
    first = place[4] == 0
    low = jnp.where(first, own[...], other[...])
    high = jnp.where(first, other[...], own[...])
    for kind, out in enumerate(outs):
        out[:, :256] = low[:, kind * 256 : kind * 256 + 256]
        out[:, 256:] = high[:, kind * 256 : kind * 256 + 256]


def shift(t, axis, by):
    n = lax.axis_size(axis)
    return lax.ppermute(t, axis, [(i, (i + by) % n) for i in range(n)])


def ring(t, axis):
    before, after = shift(t, axis, 1), shift(t, axis, -1)
    half = t.shape[0] // 2
    return t, before, after, shift(before[:half], axis, 1), shift(after[half:], axis, -1)


def stacked(blocks):
    own, before, after, far_a, far_b = blocks
    return jnp.stack([own, before, after, jnp.concatenate([far_a, far_b], axis=0)])


def exchange(t, axis):
    return lax.all_to_all(t, axis, 0, 0, tiled=True)


def main(place, tokens, cots, pieces):
    return pl.pallas_call(
        main_kernel,
        out_shape=[
            jax.ShapeDtypeStruct((4, 512, 512), BF16),
            jax.ShapeDtypeStruct((512, 1024), BF16),
        ],
        in_specs=[pl.BlockSpec(memory_space=pltpu.SMEM)] + [VMEM] * 2 + [HBM] * 10,
        out_specs=[VMEM] * 2,
        scratch_shapes=[
            pltpu.VMEM((2, 4, 2, 4, 32, 1024), BF16),
            pltpu.VMEM((32, 2, 8, 1024), F32),
            pltpu.VMEM((32, 2, 8, 1024), F32),
            pltpu.SemaphoreType.DMA((32,)),
        ],
        compiler_params=pltpu.CompilerParams(vmem_limit_bytes=LIMIT),
        cost_estimate=pl.CostEstimate(flops=4_000_000_000, bytes_accessed=11 << 20, transcendentals=1 << 18),
    )(place, tokens, cots, *pieces)


def local(kernel, shapes, scratch=(), kinds=None, limit=16):
    kinds = kinds or (BF16,) * len(shapes)

    def call(place, *arrays):
        return pl.pallas_call(
            kernel,
            out_shape=[jax.ShapeDtypeStruct(s, d) for s, d in zip(shapes, kinds)],
            in_specs=[pl.BlockSpec(memory_space=pltpu.SMEM)] + [VMEM] * len(arrays),
            out_specs=[VMEM] * len(shapes),
            scratch_shapes=list(scratch),
            compiler_params=pltpu.CompilerParams(vmem_limit_bytes=limit << 20),
            cost_estimate=pl.CostEstimate(flops=1 << 20, bytes_accessed=1 << 20, transcendentals=0),
        )(place, *arrays)

    return call


def plus(*terms):
    return sum(t.astype(F32) for t in terms).astype(BF16)


def swapped(blocks, axis):
    return [blocks[0]] + [shift(b, axis, o) for b, o in zip(blocks[1:], OFFSETS[1:])]


def on_device(frames_in, w_query, w_key, w_value, w_out, grad_in):
    together = lax.optimization_barrier
    first_core = lax.axis_index("dp") == 0
    w = jnp.stack([w_query, w_key, w_value, w_out.T], axis=1)
    w = w.reshape(32, 4, 2, 256).transpose(2, 0, 1, 3).reshape(2, 32, 1024)
    own = jnp.where(first_core, w[0], w[1])
    other = shift(jnp.where(first_core, w[1], w[0]), "dp", 1)
    w = jnp.stack([jnp.where(first_core, own, other), jnp.where(first_core, other, own)])
    other = shift(w, "z", 1)
    low = lax.axis_index("z") == 0
    pair = jnp.stack([jnp.where(low, w, other), jnp.where(low, other, w)], axis=1)
    first, second = stacked(ring(pair[0], "y")), stacked(ring(pair[1], "x"))
    u0 = exchange(grad_in.reshape(32, 16, 2048), SEQ)
    u0, first, second, frames_in = together((u0, first, second, frames_in))

    x0 = exchange(frames_in.reshape(32, 16, 2048), SEQ)
    u1 = shift(u0, "dp", 1)
    pieces = ring(first, "x") + ring(second, "y")
    x0, u1, pieces = together((x0, u1, pieces))

    x1 = shift(x0, "dp", 1)
    place = jnp.stack([lax.axis_index(a) for a in ("y", "x", "z", "heads", "dp")]).astype(jnp.int32)
    t0, d0 = main(place, x0, u0, pieces)
    x1, t0 = together((x1, t0))
    t1, d1 = main(place, x1, u1, pieces)
    t1 = shift(t1, "dp", 1)

    shapes = [(4, 2, 32, 1024)] * 3 + [(2, 2, 32, 1024)] * 2
    sources = (x0, x1, u0, u1, d0, d1)
    first = local(first_kernel, shapes, [pltpu.VMEM((4, 2, 4, 32, 1024), BF16)], limit=28)(place, *sources)
    t1, first = together((t1, first))
    term, sources = together((plus(t0, t1), sources))
    mine = lax.psum_scatter(term, "heads", scatter_dimension=0, tiled=True)
    second = local(second_kernel, shapes, limit=28)(place, *sources)
    far = [shift(first[3], "x", 1), shift(first[4], "x", -1), shift(second[3], "y", 1), shift(second[4], "y", -1)]
    near = local(far_kernel, [(4, 2, 32, 1024)] * 4)(place, *first[1:3], *far[:2], *second[1:3], *far[2:])
    blocks = [first[0], shift(near[0], "x", -1), shift(near[1], "x", 1)]
    blocks += [second[0], shift(near[2], "y", -1), shift(near[3], "y", 1)]
    blocks = local(sum_kernel, [(2, 32, 1024)] * 8)(place, *blocks)
    first, second = blocks[:4], blocks[4:]
    blocks = swapped(first, "y") + swapped(second, "x")
    keep, send = local(last_kernel, [(2, 32, 1024)] * 2, kinds=(F32, BF16))(place, *blocks)
    send = shift(send, "z", 1)
    mine, keep, send = together((mine, keep, send))
    grad_frames = exchange(mine.reshape(32, 16, 512), SEQ).reshape(1, 1, 512, 512)
    sums = (keep + send.astype(F32)) * 32768 ** (-0.5)
    sums = sums.astype(BF16)
    own = jnp.where(first_core, sums[0], sums[1])
    other = shift(jnp.where(first_core, sums[1], sums[0]), "dp", 1)
    gq, gk, gv, go = local(finish_kernel, [(32, 512)] * 4)(place, own, other)
    return grad_frames, gq, gk, gv, go.T


def solution(mesh):
    fine = Mesh(mesh.devices.reshape(2, 4, 2, 4, 4), ("dp", "y", "z", "x", "heads"))
    tokens = P("dp", SEQ, None, None)
    rows = P(("dp",) + SEQ, "heads")
    cols = P("heads", ("dp",) + SEQ)
    return jax.shard_map(
        on_device,
        mesh=fine,
        in_specs=(tokens, rows, rows, rows, cols, tokens),
        out_specs=(P("dp", SEQ, None, "heads"), rows, rows, rows, cols),
        check_vma=False,
    )
```

```python
import functools

import jax
import jax.numpy as jnp
from jax import lax
from jax.experimental import pallas as pl
from jax.experimental.pallas import tpu as pltpu
from jax.sharding import Mesh
from jax.sharding import PartitionSpec as P

HD = 128
EPS = 1e-06
FACTOR = HD ** (-0.5)
SEQ = ("y", "z", "x")
OFFSETS = (0, -1, 1, 2)
BF16 = jnp.bfloat16
F32 = jnp.float32
VMEM = pl.BlockSpec(memory_space=pltpu.VMEM)
HBM = pl.BlockSpec(memory_space=pltpu.HBM)
LIMIT = 60 * 1024 * 1024


def dot(left, right, dims):
    return lax.dot_general(left, right, (dims, ((), ())), preferred_element_type=F32)


def normed(t):
    scale = lax.rsqrt(jnp.mean(t * t, axis=-1, keepdims=True) + EPS)
    return t * scale, scale


def norm_back(n, scale, grad):
    return scale * (grad - n * jnp.mean(n * grad, axis=-1, keepdims=True))


def attention(q, k, v, g, same):
    nq, rq = normed(q)
    nk, rk = normed(k)
    nqb, nkb, vb, gb = nq.astype(BF16), nk.astype(BF16), v.astype(BF16), g.astype(BF16)
    scores = dot(nqb, nkb, ((1,), (1,))) * FACTOR
    weights = jnp.where(same, jnp.exp(scores), 0.0)
    probs = weights / jnp.sum(weights, axis=-1, keepdims=True)
    probs_b = probs.astype(BF16)
    att = dot(probs_b, vb, ((1,), (0,)))
    dprobs = dot(gb, vb, ((1,), (1,)))
    weighted = probs * dprobs
    delta = jnp.sum(weighted, axis=-1, keepdims=True)
    dscores = (weighted - probs * delta).astype(BF16)
    dnq = dot(dscores, nkb, ((1,), (0,))) * FACTOR
    dnk = dot(dscores, nqb, ((0,), (0,))) * FACTOR
    dv = dot(probs_b, gb, ((0,), (0,)))
    return norm_back(nq, rq, dnq), norm_back(nk, rk, dnk), dv, att


def main_kernel(place, x_in, u_in, *refs):
    pieces, (t_out, d_out), (w, proj, back, sems) = refs[:10], refs[10:12], refs[12:]
    y, x = place[0], place[1]
    copies = []

    def fetch(src, dst):
        copies.append(pltpu.make_async_copy(src, dst, sems.at[len(copies)]))
        copies[-1].start()

    for half in range(2):
        own, before, after, far_a, far_b = pieces[5 * half : 5 * half + 5]
        for i, outer in enumerate(OFFSETS):
            for j, inner in enumerate(OFFSETS):
                if i < 3:
                    src = (own, before, after)[i].at[j]
                else:
                    src = (far_a if j < 2 else far_b).at[j % 2]
                yy, xx = (inner, outer) if half == 0 else (outer, inner)
                fetch(src, w.at[half, lax.rem(y + yy + 4, 4), :, lax.rem(x + xx + 4, 4)])
    for copy in copies:
        copy.wait()

    row = lax.broadcasted_iota(jnp.int32, (256, 256), 0)
    col = lax.broadcasted_iota(jnp.int32, (256, 256), 1)
    same = lax.rem(row, 8) == lax.rem(col, 8)
    for kind in range(4):
        tokens = (u_in if kind == 3 else x_in)[...].reshape(512, 2048)
        cols = slice(kind * 256, kind * 256 + 256)
        acc = dot(tokens[:, :1024], w[0, :, :, :, :, cols].reshape(1024, 256), ((1,), (0,)))
        acc += dot(tokens[:, 1024:], w[1, :, :, :, :, cols].reshape(1024, 256), ((1,), (0,)))
        proj[:, :, :, cols] = acc.reshape(32, 2, 8, 256)
    for head in range(2):
        for part in range(2):
            at = [kind * 256 + head * 128 for kind in range(4)]
            out = attention(*(proj[:, part, :, a : a + 128].reshape(256, 128) for a in at), same)
            for a, value in zip(at, out):
                back[:, part, :, a : a + 128] = value.reshape(32, 8, 128)
    d_all = back[...].reshape(512, 1024).astype(BF16)
    d_out[...] = d_all
    for chunk in range(4):
        half, first = chunk // 2, 2 * (chunk % 2)
        rows = w[half, first : first + 2, :, :, :, :768].reshape(512, 768)
        t_out[chunk] = dot(d_all[:, :768], rows, ((1,), (1,))).astype(BF16)


def grads_block(place, x0, x1, u0, u1, d0, d1, cols):
    for a, b, lo, hi in ((x0, x1, 0, 768), (u0, u1, 768, 1024)):
        acc = dot(a[:, :, cols].reshape(512, 256), d0[:, lo:hi], ((0,), (0,)))
        acc += dot(b[:, :, cols].reshape(512, 256), d1[:, lo:hi], ((0,), (0,)))
        yield lo, hi, acc.reshape(2, 4, 32, hi - lo).astype(BF16)


def first_kernel(place, *refs):
    outs, full = refs[6:11], refs[11]
    for y in range(4):
        for lo, hi, rows in grads_block(place, *refs[:6], slice(y * 256, y * 256 + 256)):
            full[y, :, :, :, lo:hi] = rows
    for k in range(3):
        outs[k][...] = full[:, :, lax.rem(place[1] + OFFSETS[k] + 4, 4)]
    far = lax.rem(place[1] + 2, 4)
    outs[3][...] = full[:2, :, far]
    outs[4][...] = full[2:, :, far]


def second_kernel(place, *refs):
    outs = refs[6:11]
    for k, offset in enumerate(OFFSETS):
        start = 1024 + 256 * lax.rem(place[0] + offset + 4, 4)
        for lo, hi, rows in grads_block(place, *refs[:6], pl.ds(pl.multiple_of(start, 256), 256)):
            for x in range(4):
                out = outs[k].at[x] if k < 3 else outs[3 + x // 2].at[x % 2]
                out[:, :, lo:hi] = rows[:, x]


def far_kernel(place, *refs):
    for half in range(2):
        before, after, far_a, far_b = refs[4 * half : 4 * half + 4]
        before_out, after_out = refs[8 + 2 * half : 10 + 2 * half]
        after_out[:2] = (after[:2].astype(F32) + far_a[...].astype(F32)).astype(BF16)
        after_out[2:] = after[2:]
        before_out[:2] = before[:2]
        before_out[2:] = (before[2:].astype(F32) + far_b[...].astype(F32)).astype(BF16)


def sum_kernel(place, *refs):
    for half in range(2):
        blocks, outs = refs[3 * half : 3 * half + 3], refs[6 + 4 * half : 10 + 4 * half]
        for k, offset in enumerate(OFFSETS):
            at = lax.rem(place[half] + offset + 4, 4)
            outs[k][...] = sum(block[at].astype(F32) for block in blocks).astype(BF16)


def last_kernel(place, *refs):
    keep, send = refs[8:]
    for half in range(2):
        blocks = refs[4 * half : 4 * half + 4]
        keep[half] = sum(block[place[2]].astype(F32) for block in blocks)
        send[half] = sum(block[1 - place[2]].astype(F32) for block in blocks).astype(BF16)


def finish_kernel(place, own, other, *outs):
    first = place[4] == 0
    low = jnp.where(first, own[...], other[...])
    high = jnp.where(first, other[...], own[...])
    for kind, out in enumerate(outs):
        out[:, :256] = low[:, kind * 256 : kind * 256 + 256]
        out[:, 256:] = high[:, kind * 256 : kind * 256 + 256]


def shift(t, axis, by):
    n = lax.axis_size(axis)
    return lax.ppermute(t, axis, [(i, (i + by) % n) for i in range(n)])


def ring(t, axis):
    before, after = shift(t, axis, 1), shift(t, axis, -1)
    half = t.shape[0] // 2
    return t, before, after, shift(before[:half], axis, 1), shift(after[half:], axis, -1)


def stacked(blocks):
    own, before, after, far_a, far_b = blocks
    return jnp.stack([own, before, after, jnp.concatenate([far_a, far_b], axis=0)])


def exchange(t, axis):
    return lax.all_to_all(t, axis, 0, 0, tiled=True)


def main(place, tokens, cots, pieces):
    return pl.pallas_call(
        main_kernel,
        out_shape=[
            jax.ShapeDtypeStruct((4, 512, 512), BF16),
            jax.ShapeDtypeStruct((512, 1024), BF16),
        ],
        in_specs=[pl.BlockSpec(memory_space=pltpu.SMEM)] + [VMEM] * 2 + [HBM] * 10,
        out_specs=[VMEM] * 2,
        scratch_shapes=[
            pltpu.VMEM((2, 4, 2, 4, 32, 1024), BF16),
            pltpu.VMEM((32, 2, 8, 1024), F32),
            pltpu.VMEM((32, 2, 8, 1024), F32),
            pltpu.SemaphoreType.DMA((32,)),
        ],
        compiler_params=pltpu.CompilerParams(vmem_limit_bytes=LIMIT),
        cost_estimate=pl.CostEstimate(flops=4_000_000_000, bytes_accessed=11 << 20, transcendentals=1 << 18),
    )(place, tokens, cots, *pieces)


def local(kernel, shapes, scratch=(), kinds=None, limit=16):
    kinds = kinds or (BF16,) * len(shapes)

    def call(place, *arrays):
        return pl.pallas_call(
            kernel,
            out_shape=[jax.ShapeDtypeStruct(s, d) for s, d in zip(shapes, kinds)],
            in_specs=[pl.BlockSpec(memory_space=pltpu.SMEM)] + [VMEM] * len(arrays),
            out_specs=[VMEM] * len(shapes),
            scratch_shapes=list(scratch),
            compiler_params=pltpu.CompilerParams(vmem_limit_bytes=limit << 20),
            cost_estimate=pl.CostEstimate(flops=1 << 20, bytes_accessed=1 << 20, transcendentals=0),
        )(place, *arrays)

    return call


def plus(*terms):
    return sum(t.astype(F32) for t in terms).astype(BF16)


def swapped(blocks, axis):
    return [blocks[0]] + [shift(b, axis, o) for b, o in zip(blocks[1:], OFFSETS[1:])]


def on_device(frames_in, w_query, w_key, w_value, w_out, grad_in):
    together = lax.optimization_barrier
    first_core = lax.axis_index("dp") == 0
    w = jnp.stack([w_query, w_key, w_value, w_out.T], axis=1)
    w = w.reshape(32, 4, 2, 256).transpose(2, 0, 1, 3).reshape(2, 32, 1024)
    own = jnp.where(first_core, w[0], w[1])
    other = shift(jnp.where(first_core, w[1], w[0]), "dp", 1)
    w = jnp.stack([jnp.where(first_core, own, other), jnp.where(first_core, other, own)])
    other = shift(w, "z", 1)
    low = lax.axis_index("z") == 0
    pair = jnp.stack([jnp.where(low, w, other), jnp.where(low, other, w)], axis=1)
    first, second = stacked(ring(pair[0], "y")), stacked(ring(pair[1], "x"))
    u0 = exchange(grad_in.reshape(32, 16, 2048), SEQ)
    u0, first, second, frames_in = together((u0, first, second, frames_in))

    x0 = exchange(frames_in.reshape(32, 16, 2048), SEQ)
    u1 = shift(u0, "dp", 1)
    pieces = ring(first, "x") + ring(second, "y")
    x0, u1, pieces = together((x0, u1, pieces))

    x1 = shift(x0, "dp", 1)
    place = jnp.stack([lax.axis_index(a) for a in ("y", "x", "z", "heads", "dp")]).astype(jnp.int32)
    t0, d0 = main(place, x0, u0, pieces)
    x1, t0 = together((x1, t0))
    t1, d1 = main(place, x1, u1, pieces)
    t1 = shift(t1, "dp", 1)

    shapes = [(4, 2, 32, 1024)] * 3 + [(2, 2, 32, 1024)] * 2
    sources = (x0, x1, u0, u1, d0, d1)
    first = local(first_kernel, shapes, [pltpu.VMEM((4, 2, 4, 32, 1024), BF16)], limit=28)(place, *sources)
    t1, first = together((t1, first))
    term, sources = together((plus(t0, t1), sources))
    mine = lax.psum_scatter(term, "heads", scatter_dimension=0, tiled=True)
    second = local(second_kernel, shapes, limit=28)(place, *sources)
    far = [shift(first[3], "x", 1), shift(first[4], "x", -1), shift(second[3], "y", 1), shift(second[4], "y", -1)]
    near = local(far_kernel, [(4, 2, 32, 1024)] * 4)(place, *first[1:3], *far[:2], *second[1:3], *far[2:])
    blocks = [first[0], shift(near[0], "x", -1), shift(near[1], "x", 1)]
    blocks += [second[0], shift(near[2], "y", -1), shift(near[3], "y", 1)]
    blocks = local(sum_kernel, [(2, 32, 1024)] * 8)(place, *blocks)
    first, second = blocks[:4], blocks[4:]
    blocks = swapped(first, "y") + swapped(second, "x")
    keep, send = local(last_kernel, [(2, 32, 1024)] * 2, kinds=(F32, BF16))(place, *blocks)
    mine, keep, send = together((mine, keep, send))
    grad_frames = exchange(mine.reshape(32, 16, 512), SEQ).reshape(1, 1, 512, 512)
    send = shift(send, "z", 1)
    sums = (keep + send.astype(F32)) * 32768 ** (-0.5)
    sums = sums.astype(BF16)
    own = jnp.where(first_core, sums[0], sums[1])
    other = shift(jnp.where(first_core, sums[1], sums[0]), "dp", 1)
    gq, gk, gv, go = local(finish_kernel, [(32, 512)] * 4)(place, own, other)
    return grad_frames, gq, gk, gv, go.T


def solution(mesh):
    fine = Mesh(mesh.devices.reshape(2, 4, 2, 4, 4), ("dp", "y", "z", "x", "heads"))
    tokens = P("dp", SEQ, None, None)
    rows = P(("dp",) + SEQ, "heads")
    cols = P("heads", ("dp",) + SEQ)
    return jax.shard_map(
        on_device,
        mesh=fine,
        in_specs=(tokens, rows, rows, rows, cols, tokens),
        out_specs=(P("dp", SEQ, None, "heads"), rows, rows, rows, cols),
        check_vma=False,
    )
```

```python
import functools

import jax
import jax.numpy as jnp
from jax import lax
from jax.experimental import pallas as pl
from jax.experimental.pallas import tpu as pltpu
from jax.sharding import Mesh
from jax.sharding import PartitionSpec as P

HD = 128
EPS = 1e-06
FACTOR = HD ** (-0.5)
SEQ = ("y", "z", "x")
OFFSETS = (0, -1, 1, 2)
BF16 = jnp.bfloat16
F32 = jnp.float32
VMEM = pl.BlockSpec(memory_space=pltpu.VMEM)
HBM = pl.BlockSpec(memory_space=pltpu.HBM)
LIMIT = 60 * 1024 * 1024


def dot(left, right, dims):
    return lax.dot_general(left, right, (dims, ((), ())), preferred_element_type=F32)


def normed(t):
    scale = lax.rsqrt(jnp.mean(t * t, axis=-1, keepdims=True) + EPS)
    return t * scale, scale


def norm_back(n, scale, grad):
    return scale * (grad - n * jnp.mean(n * grad, axis=-1, keepdims=True))


def attention(q, k, v, g, same):
    nq, rq = normed(q)
    nk, rk = normed(k)
    nqb, nkb, vb, gb = nq.astype(BF16), nk.astype(BF16), v.astype(BF16), g.astype(BF16)
    scores = dot(nqb, nkb, ((1,), (1,))) * FACTOR
    weights = jnp.where(same, jnp.exp(scores), 0.0)
    probs = weights / jnp.sum(weights, axis=-1, keepdims=True)
    probs_b = probs.astype(BF16)
    att = dot(probs_b, vb, ((1,), (0,)))
    dprobs = dot(gb, vb, ((1,), (1,)))
    weighted = probs * dprobs
    delta = jnp.sum(weighted, axis=-1, keepdims=True)
    dscores = (weighted - probs * delta).astype(BF16)
    dnq = dot(dscores, nkb, ((1,), (0,))) * FACTOR
    dnk = dot(dscores, nqb, ((0,), (0,))) * FACTOR
    dv = dot(probs_b, gb, ((0,), (0,)))
    return norm_back(nq, rq, dnq), norm_back(nk, rk, dnk), dv, att


def main_kernel(place, x_in, u_in, *refs):
    pieces, (t_out, d_out), (w, proj, back, sems) = refs[:10], refs[10:12], refs[12:]
    y, x = place[0], place[1]
    copies = []

    def fetch(src, dst):
        copies.append(pltpu.make_async_copy(src, dst, sems.at[len(copies)]))
        copies[-1].start()

    for half in range(2):
        own, before, after, far_a, far_b = pieces[5 * half : 5 * half + 5]
        for i, outer in enumerate(OFFSETS):
            for j, inner in enumerate(OFFSETS):
                if i < 3:
                    src = (own, before, after)[i].at[j]
                else:
                    src = (far_a if j < 2 else far_b).at[j % 2]
                yy, xx = (inner, outer) if half == 0 else (outer, inner)
                fetch(src, w.at[half, lax.rem(y + yy + 4, 4), :, lax.rem(x + xx + 4, 4)])
    for copy in copies:
        copy.wait()

    row = lax.broadcasted_iota(jnp.int32, (256, 256), 0)
    col = lax.broadcasted_iota(jnp.int32, (256, 256), 1)
    same = lax.rem(row, 8) == lax.rem(col, 8)
    for kind in range(4):
        tokens = (u_in if kind == 3 else x_in)[...].reshape(512, 2048)
        cols = slice(kind * 256, kind * 256 + 256)
        acc = dot(tokens[:, :1024], w[0, :, :, :, :, cols].reshape(1024, 256), ((1,), (0,)))
        acc += dot(tokens[:, 1024:], w[1, :, :, :, :, cols].reshape(1024, 256), ((1,), (0,)))
        proj[:, :, :, cols] = acc.reshape(32, 2, 8, 256)
    for head in range(2):
        for part in range(2):
            at = [kind * 256 + head * 128 for kind in range(4)]
            out = attention(*(proj[:, part, :, a : a + 128].reshape(256, 128) for a in at), same)
            for a, value in zip(at, out):
                back[:, part, :, a : a + 128] = value.reshape(32, 8, 128)
    d_all = back[...].reshape(512, 1024).astype(BF16)
    d_out[...] = d_all
    for chunk in range(4):
        half, first = chunk // 2, 2 * (chunk % 2)
        rows = w[half, first : first + 2, :, :, :, :768].reshape(512, 768)
        t_out[chunk] = dot(d_all[:, :768], rows, ((1,), (1,))).astype(BF16)


def grads_block(place, x0, x1, u0, u1, d0, d1, cols):
    for a, b, lo, hi in ((x0, x1, 0, 768), (u0, u1, 768, 1024)):
        acc = dot(a[:, :, cols].reshape(512, 256), d0[:, lo:hi], ((0,), (0,)))
        acc += dot(b[:, :, cols].reshape(512, 256), d1[:, lo:hi], ((0,), (0,)))
        yield lo, hi, acc.reshape(2, 4, 32, hi - lo).astype(BF16)


def first_kernel(place, *refs):
    outs, full = refs[6:11], refs[11]
    for y in range(4):
        for lo, hi, rows in grads_block(place, *refs[:6], slice(y * 256, y * 256 + 256)):
            full[y, :, :, :, lo:hi] = rows
    for k in range(3):
        outs[k][...] = full[:, :, lax.rem(place[1] + OFFSETS[k] + 4, 4)]
    far = lax.rem(place[1] + 2, 4)
    outs[3][...] = full[:2, :, far]
    outs[4][...] = full[2:, :, far]


def second_kernel(place, *refs):
    outs = refs[6:11]
    for k, offset in enumerate(OFFSETS):
        start = 1024 + 256 * lax.rem(place[0] + offset + 4, 4)
        for lo, hi, rows in grads_block(place, *refs[:6], pl.ds(pl.multiple_of(start, 256), 256)):
            for x in range(4):
                out = outs[k].at[x] if k < 3 else outs[3 + x // 2].at[x % 2]
                out[:, :, lo:hi] = rows[:, x]


def far_kernel(place, *refs):
    for half in range(2):
        before, after, far_a, far_b = refs[4 * half : 4 * half + 4]
        before_out, after_out = refs[8 + 2 * half : 10 + 2 * half]
        after_out[:2] = (after[:2].astype(F32) + far_a[...].astype(F32)).astype(BF16)
        after_out[2:] = after[2:]
        before_out[:2] = before[:2]
        before_out[2:] = (before[2:].astype(F32) + far_b[...].astype(F32)).astype(BF16)


def sum_kernel(place, *refs):
    for half in range(2):
        blocks, outs = refs[3 * half : 3 * half + 3], refs[6 + 4 * half : 10 + 4 * half]
        for k, offset in enumerate(OFFSETS):
            at = lax.rem(place[half] + offset + 4, 4)
            outs[k][...] = sum(block[at].astype(F32) for block in blocks).astype(BF16)


def last_kernel(place, *refs):
    keep, send = refs[8:]
    for half in range(2):
        blocks = refs[4 * half : 4 * half + 4]
        keep[half] = sum(block[place[2]].astype(F32) for block in blocks)
        send[half] = sum(block[1 - place[2]].astype(F32) for block in blocks).astype(BF16)


def finish_kernel(place, own, other, *outs):
    first = place[4] == 0
    low = jnp.where(first, own[...], other[...])
    high = jnp.where(first, other[...], own[...])
    for kind, out in enumerate(outs):
        out[:, :256] = low[:, kind * 256 : kind * 256 + 256]
        out[:, 256:] = high[:, kind * 256 : kind * 256 + 256]


def shift(t, axis, by):
    n = lax.axis_size(axis)
    return lax.ppermute(t, axis, [(i, (i + by) % n) for i in range(n)])


def ring(t, axis):
    before, after = shift(t, axis, 1), shift(t, axis, -1)
    half = t.shape[0] // 2
    return t, before, after, shift(before[:half], axis, 1), shift(after[half:], axis, -1)


def stacked(blocks):
    own, before, after, far_a, far_b = blocks
    return jnp.stack([own, before, after, jnp.concatenate([far_a, far_b], axis=0)])


def exchange(t, axis):
    return lax.all_to_all(t, axis, 0, 0, tiled=True)


def main(place, tokens, cots, pieces):
    return pl.pallas_call(
        main_kernel,
        out_shape=[
            jax.ShapeDtypeStruct((4, 512, 512), BF16),
            jax.ShapeDtypeStruct((512, 1024), BF16),
        ],
        in_specs=[pl.BlockSpec(memory_space=pltpu.SMEM)] + [VMEM] * 2 + [HBM] * 10,
        out_specs=[VMEM] * 2,
        scratch_shapes=[
            pltpu.VMEM((2, 4, 2, 4, 32, 1024), BF16),
            pltpu.VMEM((32, 2, 8, 1024), F32),
            pltpu.VMEM((32, 2, 8, 1024), F32),
            pltpu.SemaphoreType.DMA((32,)),
        ],
        compiler_params=pltpu.CompilerParams(vmem_limit_bytes=LIMIT),
        cost_estimate=pl.CostEstimate(flops=4_000_000_000, bytes_accessed=11 << 20, transcendentals=1 << 18),
    )(place, tokens, cots, *pieces)


def local(kernel, shapes, scratch=(), kinds=None, limit=16):
    kinds = kinds or (BF16,) * len(shapes)

    def call(place, *arrays):
        return pl.pallas_call(
            kernel,
            out_shape=[jax.ShapeDtypeStruct(s, d) for s, d in zip(shapes, kinds)],
            in_specs=[pl.BlockSpec(memory_space=pltpu.SMEM)] + [VMEM] * len(arrays),
            out_specs=[VMEM] * len(shapes),
            scratch_shapes=list(scratch),
            compiler_params=pltpu.CompilerParams(vmem_limit_bytes=limit << 20),
            cost_estimate=pl.CostEstimate(flops=1 << 20, bytes_accessed=1 << 20, transcendentals=0),
        )(place, *arrays)

    return call


def plus(*terms):
    return sum(t.astype(F32) for t in terms).astype(BF16)


def swapped(blocks, axis):
    return [blocks[0]] + [shift(b, axis, o) for b, o in zip(blocks[1:], OFFSETS[1:])]


def on_device(frames_in, w_query, w_key, w_value, w_out, grad_in):
    together = lax.optimization_barrier
    first_core = lax.axis_index("dp") == 0
    w = jnp.stack([w_query, w_key, w_value, w_out.T], axis=1)
    w = w.reshape(32, 4, 2, 256).transpose(2, 0, 1, 3).reshape(2, 32, 1024)
    own = jnp.where(first_core, w[0], w[1])
    other = shift(jnp.where(first_core, w[1], w[0]), "dp", 1)
    w = jnp.stack([jnp.where(first_core, own, other), jnp.where(first_core, other, own)])
    other = shift(w, "z", 1)
    low = lax.axis_index("z") == 0
    pair = jnp.stack([jnp.where(low, w, other), jnp.where(low, other, w)], axis=1)
    first, second = stacked(ring(pair[0], "y")), stacked(ring(pair[1], "x"))
    u0 = exchange(grad_in.reshape(32, 16, 2048), SEQ)
    place = jnp.stack([lax.axis_index(a) for a in ("y", "x", "z", "heads", "dp")]).astype(jnp.int32)
    u0, first, second, frames_in, place = together((u0, first, second, frames_in, place))

    x0 = exchange(frames_in.reshape(32, 16, 2048), SEQ)
    u1 = shift(u0, "dp", 1)
    pieces = ring(first, "x") + ring(second, "y")
    x0, u1, pieces = together((x0, u1, pieces))

    x1 = shift(x0, "dp", 1)
    t0, d0 = main(place, x0, u0, pieces)
    x1, t0 = together((x1, t0))
    t1, d1 = main(place, x1, u1, pieces)
    t1 = shift(t1, "dp", 1)

    shapes = [(4, 2, 32, 1024)] * 3 + [(2, 2, 32, 1024)] * 2
    sources = (x0, x1, u0, u1, d0, d1)
    first = local(first_kernel, shapes, [pltpu.VMEM((4, 2, 4, 32, 1024), BF16)], limit=28)(place, *sources)
    term, sources = together((plus(t0, t1), sources))
    mine = lax.psum_scatter(term, "heads", scatter_dimension=0, tiled=True)
    second = local(second_kernel, shapes, limit=28)(place, *sources)
    far = [shift(first[3], "x", 1), shift(first[4], "x", -1), shift(second[3], "y", 1), shift(second[4], "y", -1)]
    near = local(far_kernel, [(4, 2, 32, 1024)] * 4)(place, *first[1:3], *far[:2], *second[1:3], *far[2:])
    blocks = [first[0], shift(near[0], "x", -1), shift(near[1], "x", 1)]
    blocks += [second[0], shift(near[2], "y", -1), shift(near[3], "y", 1)]
    blocks = local(sum_kernel, [(2, 32, 1024)] * 8)(place, *blocks)
    first, second = blocks[:4], blocks[4:]
    blocks = swapped(first, "y") + swapped(second, "x")
    keep, send = local(last_kernel, [(2, 32, 1024)] * 2, kinds=(F32, BF16))(place, *blocks)
    mine, keep, send = together((mine, keep, send))
    grad_frames = exchange(mine.reshape(32, 16, 512), SEQ).reshape(1, 1, 512, 512)
    send = shift(send, "z", 1)
    sums = (keep + send.astype(F32)) * 32768 ** (-0.5)
    sums = sums.astype(BF16)
    own = jnp.where(first_core, sums[0], sums[1])
    other = shift(jnp.where(first_core, sums[1], sums[0]), "dp", 1)
    gq, gk, gv, go = local(finish_kernel, [(32, 512)] * 4)(place, own, other)
    return grad_frames, gq, gk, gv, go.T


def solution(mesh):
    fine = Mesh(mesh.devices.reshape(2, 4, 2, 4, 4), ("dp", "y", "z", "x", "heads"))
    tokens = P("dp", SEQ, None, None)
    rows = P(("dp",) + SEQ, "heads")
    cols = P("heads", ("dp",) + SEQ)
    return jax.shard_map(
        on_device,
        mesh=fine,
        in_specs=(tokens, rows, rows, rows, cols, tokens),
        out_specs=(P("dp", SEQ, None, "heads"), rows, rows, rows, cols),
        check_vma=False,
    )
```
